1024 devices in a mesh: users: 64 (over x, z), items: 16 (over y, core).
Axes of the slice: x: 4, y: 8, z: 16, core: 2. Of those that a mesh axis runs over, the one named last changes fastest.
Arguments:
- user_factors: bfloat16 [16384, 256], P('users'), may hold values from -1.5 to 1.5
- item_factors: bfloat16 [32768, 256], P('items'), may hold values from -1.5 to 1.5
- pattern: int32 [128, 16, 16], P('users', 'items'), may hold values from 0 to 15
- counts: int32 [128, 16], P('users', 'items'), may hold values from 1 to 16, as said below
- confidence: bfloat16 [128, 16, 16, 128, 128], P('users', 'items'), may hold values from 0 to 16, as said below
Outputs:
- user_gradient: float32 [16384, 256], P(('users', 'items'))
- item_gradient: float32 [16, 2048, 256], P('items', 'users')
The draws below stay inside these ranges and needn't reach their ends.
Inputs may be any that keep to these rules, and one draw needn't show every extreme that they name: `counts`: every user tile has 16 live slots in one item shard. `confidence`: about half of the entries are zero.
All inputs are finite; a program needn't handle non-finite values.
Results may differ from the reference program's by a relative error of at most 0.00098.
Values sent between devices are 32-bit elements; how exact they have to be, the bound alone decides.
No kernel may reach another device: no remote copies, remote signals or barrier semaphores. Data moves between devices by JAX's collectives and lax.ppermute only.
A program may use at most 32 MiB of HBM per device.

```python
import jax
import jax.numpy as jnp
from jax import lax

K = 256
TILE = 128
IT_DEV = 16
SLOTS = 16
USER_TILES = 128
USERS = 16384
ISHARD = 2048
ITEMS = 32768
N_ITEMS = 16


def draw_counts(key, part):
    key = jax.random.fold_in(key, 11)
    base = jax.random.randint(key, (USER_TILES, N_ITEMS), 1, SLOTS + 1)
    tile_ids = jnp.arange(USER_TILES, dtype=jnp.int32)[:, None]
    shard_ids = jnp.arange(N_ITEMS, dtype=jnp.int32)[None, :]
    full_slot = tile_ids % N_ITEMS == shard_ids
    return jnp.where(full_slot, SLOTS, base).astype(jnp.int32)


def draw_confidence(key, part):
    key = jax.random.fold_in(key, 12)
    key_keep, key_vals = jax.random.split(key)
    shape = (USER_TILES, N_ITEMS, SLOTS, TILE, TILE)
    keep = jax.random.bernoulli(key_keep, 0.5, shape).astype(jnp.float32)
    values = jnp.exp(jax.random.uniform(key_vals, shape, jnp.float32, jnp.log(0.5), jnp.log(8.0)))
    return (keep * values).astype(jnp.bfloat16)


def with_ends(values, key, low, top_value):
    shape = values.shape
    place = [jax.random.randint(jax.random.fold_in(key, axis), (), 0, shape[axis]) for axis in range(len(shape))]
    values = values.at[tuple(place)].set(low)
    longest = shape.index(max(shape))
    place[longest] = (place[longest] + 1) % shape[longest]
    return values.at[tuple(place)].set(top_value)


def levels(rng, extent, cuts, least, top_value):
    level = 1.0
    for position, shards_of in cuts:
        steps = jax.random.uniform(jax.random.fold_in(jax.random.fold_in(rng, 6), position), (shards_of,), jnp.float32, least / len(cuts), top_value / len(cuts))
        level = level * jnp.repeat(jnp.exp(steps), extent[position] // shards_of).reshape((-1,) + (1,) * (len(extent) - 1 - position))
    return level


def gaussian(own_key, extent, spread, limit, shards=(), held_as=jnp.bfloat16):
    result = spread * jax.random.normal(own_key, extent, jnp.float32)
    if shards:
        result = result * levels(own_key, extent, shards, -0.22, 0.18)
    return jnp.clip(result, -limit, limit).astype(held_as)


def setup_inputs(seed: int = 0) -> dict:
    key_of = jax.random.split(jax.random.key(seed), 6)
    return {
        "user_factors": gaussian(key_of[0], (USERS, K), 0.25, 1.5, ((0, 64),)),
        "item_factors": gaussian(key_of[1], (ITEMS, K), 0.25, 1.5, ((0, 16),)),
        "pattern": with_ends(jax.random.randint(key_of[2], (USER_TILES, N_ITEMS, SLOTS), 0, IT_DEV), jax.random.fold_in(key_of[2], 1), 0, IT_DEV - 1).astype(jnp.int32),
        "counts": draw_counts(jax.random.fold_in(key_of[5], 71), 0),
        "confidence": draw_confidence(jax.random.fold_in(key_of[5], 71), 0),
    }


WEIGHT_ALL = 8.0
RIDGE_COEF = 0.5


def reference(user_factors, item_factors, pattern, counts, confidence):
    gram_x = jnp.dot(user_factors.T, user_factors, preferred_element_type=jnp.float32)
    gram_y = jnp.dot(item_factors.T, item_factors, preferred_element_type=jnp.float32)
    item_tiles = item_factors.reshape(N_ITEMS, IT_DEV, TILE, K)
    shard_ids = jnp.arange(N_ITEMS, dtype=jnp.int32)[:, None]
    slot_ids = jnp.arange(SLOTS, dtype=jnp.int32)[None, :]
    highest = lax.Precision.HIGHEST

    def step(accum, inputs):
        user_tile, chosen, live_count, conf = inputs
        picked = item_tiles[shard_ids, chosen].astype(jnp.float32)
        user_f = user_tile.astype(jnp.float32)
        scores = jnp.einsum('ak,jsck->jsac', user_f, picked, precision=highest)
        live = (slot_ids < live_count[:, None]).astype(jnp.float32)
        residual_tiles = (live[:, :, None, None] * conf.astype(jnp.float32) * (scores - 1.0)).astype(jnp.bfloat16)
        res_f = residual_tiles.astype(jnp.float32)
        user_part = jnp.einsum('jsac,jsck->ak', res_f, picked, precision=highest)
        contrib = jnp.einsum('jsac,ak->jsck', res_f, user_f, precision=highest)
        accum = accum.at[shard_ids, chosen].add(contrib)
        return accum, user_part

    user_tiles = user_factors.reshape(USER_TILES, TILE, K)
    start = jnp.zeros((N_ITEMS, IT_DEV, TILE, K), jnp.float32)
    accum, user_parts = lax.scan(step, start, (user_tiles, pattern, counts, confidence))
    user_sum = user_parts.reshape(USERS, K)
    item_sum = accum.reshape(ITEMS, K)
    user_f = user_factors.astype(jnp.float32)
    item_f = item_factors.astype(jnp.float32)
    norm_user = float(SLOTS * N_ITEMS * TILE) ** 0.5
    norm_item = float(USERS * SLOTS / IT_DEV) ** 0.5
    user_gradient = 2.0 * (WEIGHT_ALL * jnp.dot(user_f, gram_y, precision=highest) / ITEMS + user_sum / norm_user + RIDGE_COEF * user_f)
    item_gradient = 2.0 * (WEIGHT_ALL * jnp.dot(item_f, gram_x, precision=highest) / USERS + item_sum / norm_item + RIDGE_COEF * item_f)
    return user_gradient, item_gradient.reshape(N_ITEMS, ISHARD, K)
```

```python
import math

import jax
import jax.numpy as jnp
from jax import lax
from jax.experimental import pallas as pl
from jax.experimental.pallas import tpu as pltpu
from jax.sharding import Mesh, PartitionSpec as P

WEIGHT_ALL = 8.0
RIDGE_COEF = 0.5
F32 = jnp.float32
BF16 = jnp.bfloat16


def dot(a, b, dims):
    return lax.dot_general(a, b, (dims, ((), ())), preferred_element_type=F32)


def split(a):
    high = a.astype(BF16)
    return high, (a - high.astype(F32)).astype(BF16)


def local_kernel(item_scale, item_gram, user_scale, user_gram,
                 pat, cnt, x_ref, y_ref, c_ref, item_ref, user_ref, s_ref, w_ref):
    user_tiles, slots, tile, _ = c_ref.shape
    item_tiles = y_ref.shape[0] // tile
    x = x_ref[...]
    for t in range(item_tiles):
        y_t = y_ref[t * tile:(t + 1) * tile, :]
        s_ref[t] = dot(x, y_t, ((1,), (1,))) - 1.0
        w_ref[t] = jnp.zeros_like(w_ref[t])
    for b in range(user_tiles):
        rows = pl.ds(b * tile, tile)
        for s in range(slots):
            @pl.when(s < cnt[b, 0])
            def _():
                t = pat[b, s]
                residual = (c_ref[b, s].astype(F32) * s_ref[t, rows, :]).astype(BF16)
                w_ref[t, rows, :] += residual.astype(F32)
    gx_high, gx_low = split(dot(x, x, ((0,), (0,))) * item_gram)
    y = y_ref[...]
    gy_high, gy_low = split(dot(y, y, ((0,), (0,))) * user_gram)
    user = jnp.zeros(user_ref.shape, F32)
    for t in range(item_tiles):
        y_t = y_ref[t * tile:(t + 1) * tile, :]
        high, low = split(w_ref[t])
        user += dot(high, y_t, ((1,), (0,))) + dot(low, y_t, ((1,), (0,)))
        part = dot(high, x, ((0,), (0,))) + dot(low, x, ((0,), (0,)))
        gram = dot(y_t, gx_high, ((1,), (0,))) + dot(y_t, gx_low, ((1,), (0,)))
        item_ref[t * tile:(t + 1) * tile, :] = part * item_scale + gram
    gram = dot(x, gy_high, ((1,), (0,))) + dot(x, gy_low, ((1,), (0,)))
    user_ref[...] = user * user_scale + gram


def shards(user_factors, item_factors, pattern, counts, confidence):
    user_size = lax.axis_size(("x", "z"))
    item_size = lax.axis_size(("y", "core"))
    user_index = lax.axis_index(("x", "z"))
    item_index = lax.axis_index(("y", "core"))
    user_rows, feat_width = user_factors.shape
    item_rows = item_factors.shape[0]
    tile_rows = confidence.shape[-1]
    slot_count = pattern.shape[-1]
    user_tiles = user_rows // tile_rows
    item_tiles = item_rows // tile_rows
    users_total = user_rows * user_size
    items_total = item_rows * item_size
    share_rows = user_rows // item_size
    owner_rows = item_rows // user_size
    norm_user = math.sqrt(slot_count * item_size * tile_rows)
    norm_item = math.sqrt(users_total * slot_count / item_tiles)

    item_part, user_part = pl.pallas_call(
        lambda *refs: local_kernel(
            2.0 / norm_item, 2.0 * WEIGHT_ALL / users_total,
            2.0 / norm_user, 2.0 * WEIGHT_ALL / items_total, *refs),
        out_shape=(
            jax.ShapeDtypeStruct((item_rows, feat_width), F32),
            jax.ShapeDtypeStruct((user_rows, feat_width), F32),
        ),
        in_specs=[
            pl.BlockSpec(memory_space=pltpu.SMEM),
            pl.BlockSpec(memory_space=pltpu.SMEM),
            pl.BlockSpec(memory_space=pltpu.VMEM),
            pl.BlockSpec(memory_space=pltpu.VMEM),
            pl.BlockSpec(memory_space=pltpu.VMEM),
        ],
        out_specs=(
            pl.BlockSpec(memory_space=pltpu.VMEM),
            pl.BlockSpec(memory_space=pltpu.VMEM),
        ),
        scratch_shapes=[
            pltpu.VMEM((item_tiles, user_rows, tile_rows), F32),
            pltpu.VMEM((item_tiles, user_rows, tile_rows), F32),
        ],
        compiler_params=pltpu.CompilerParams(vmem_limit_bytes=32 * 1024 * 1024),
        name="local_sums",
    )(pattern[:, 0, :], counts, user_factors, item_factors, confidence[:, 0])

    def reduce_over(part, axes):
        size = lax.axis_size(axes)
        moved = lax.all_to_all(part, axes, 0, 0, tiled=True)
        return moved.reshape(size, part.shape[0] // size, feat_width).sum(0)

    item_x = reduce_over(item_part, "x")
    user_share = reduce_over(user_part, ("y", "core"))
    item_share = reduce_over(item_x, "z")

    own_user = lax.dynamic_slice_in_dim(user_factors, item_index * share_rows, share_rows, 0)
    own_item = lax.dynamic_slice_in_dim(item_factors, user_index * owner_rows, owner_rows, 0)
    user_gradient = user_share + 2.0 * RIDGE_COEF * own_user.astype(F32)
    item_gradient = item_share + 2.0 * RIDGE_COEF * own_item.astype(F32)
    return (user_gradient, item_gradient[None])


def solution(mesh):
    fine = Mesh(mesh.devices.reshape(4, 16, 8, 2), ("x", "z", "y", "core"))
    users, items = ("x", "z"), ("y", "core")
    return jax.shard_map(
        shards,
        mesh=fine,
        in_specs=(
            P(users, None),
            P(items, None),
            P(users, items, None),
            P(users, items),
            P(users, items, None, None, None),
        ),
        out_specs=(P(users + items, None), P(items, users, None)),
        check_vma=False,
    )
```

```python
import math

import jax
import jax.numpy as jnp
from jax import lax
from jax.experimental import pallas as pl
from jax.experimental.pallas import tpu as pltpu
from jax.sharding import Mesh, PartitionSpec as P

WEIGHT_ALL = 8.0
RIDGE_COEF = 0.5
F32 = jnp.float32
BF16 = jnp.bfloat16
USERS = ("x", "zh", "zl")
ITEMS = ("y", "core")


def dot(a, b, dims):
    return lax.dot_general(a, b, (dims, ((), ())), preferred_element_type=F32)


def split(a):
    high = a.astype(BF16)
    return high, (a - high.astype(F32)).astype(BF16)


def eye(n, value):
    row = lax.broadcasted_iota(jnp.int32, (n, n), 0)
    col = lax.broadcasted_iota(jnp.int32, (n, n), 1)
    return jnp.where(row == col, value, 0.0).astype(F32)


def local_kernel(scales, sizes, x_hbm, y_hbm, c_hbm, pat_hbm, cnt_hbm, item_ref, user_ref,
                 x_ref, y_ref, c_ref, pat, cnt, s_ref, w_ref, sems):
    item_scale, item_gram, item_ridge, user_scale, user_gram, user_ridge = scales
    x_size, zh_size, zl_size = sizes
    user_tiles, _, slots, tile, _ = c_ref.shape
    width = x_ref.shape[1]
    item_rows = y_ref.shape[0]
    item_tiles = item_rows // tile
    owner_rows = item_rows // (x_size * zh_size * zl_size)
    block = min(tile, owner_rows)
    copies = [
        pltpu.make_async_copy(src, dst, sems.at[k])
        for k, (src, dst) in enumerate(
            ((x_hbm, x_ref), (y_hbm, y_ref), (pat_hbm, pat), (cnt_hbm, cnt), (c_hbm, c_ref)))
    ]
    for copy in copies:
        copy.start()
    w_ref[...] = jnp.zeros_like(w_ref)
    copies[0].wait()
    copies[1].wait()
    x = x_ref[...]
    for t in range(item_tiles):
        s_ref[t] = dot(x, y_ref[t * tile:(t + 1) * tile, :], ((1,), (1,))) - 1.0
    for copy in copies[2:]:
        copy.wait()
    for b in range(user_tiles):
        rows = pl.ds(b * tile, tile)
        for s in range(slots):
            t = pat[b, 0, s]
            live = jnp.where(s < cnt[0, b], 1.0, 0.0).astype(F32)
            residual = (live * c_ref[b, 0, s].astype(F32) * s_ref[t, rows, :]).astype(BF16)
            w_ref[t, rows, :] += residual.astype(F32)
    gx_high, gx_low = split(dot(x, x, ((0,), (0,))) * item_gram + eye(width, item_ridge))
    y = y_ref[...]
    gy_high, gy_low = split(dot(y, y, ((0,), (0,))) * user_gram + eye(width, user_ridge))
    user = jnp.zeros(user_ref.shape, F32)
    for t in range(item_tiles):
        y_t = y_ref[t * tile:(t + 1) * tile, :]
        high, low = split(w_ref[t])
        user += dot(high, y_t, ((1,), (0,))) + dot(low, y_t, ((1,), (0,)))
        part = dot(high, x, ((0,), (0,))) + dot(low, x, ((0,), (0,)))
        gram = dot(y_t, gx_high, ((1,), (0,))) + dot(y_t, gx_low, ((1,), (0,)))
        whole = part * item_scale + gram
        for k in range(0, tile, block):
            owner, offset = divmod(t * tile + k, owner_rows)
            xi, zh, zl = owner // (zh_size * zl_size), owner // zl_size % zh_size, owner % zl_size
            place = ((xi * zl_size + zl) * zh_size + zh) * owner_rows + offset
            item_ref[place:place + block, :] = whole[k:k + block, :]
    gram = dot(x, gy_high, ((1,), (0,))) + dot(x, gy_low, ((1,), (0,)))
    user_ref[...] = user * user_scale + gram


def shards(user_factors, item_factors, pattern, counts, confidence):
    user_size = lax.axis_size(USERS)
    item_size = lax.axis_size(ITEMS)
    user_rows, feat_width = user_factors.shape
    item_rows = item_factors.shape[0]
    tile_rows = confidence.shape[-1]
    slot_count = pattern.shape[-1]
    user_tiles = user_rows // tile_rows
    item_tiles = item_rows // tile_rows
    users_total = user_rows * user_size
    items_total = item_rows * item_size
    norm_user = math.sqrt(slot_count * item_size * tile_rows)
    norm_item = math.sqrt(users_total * slot_count / item_tiles)
    scales = (
        2.0 / norm_item, 2.0 * WEIGHT_ALL / users_total, 2.0 * RIDGE_COEF / user_size,
        2.0 / norm_user, 2.0 * WEIGHT_ALL / items_total, 2.0 * RIDGE_COEF / item_size,
    )
    sizes = tuple(lax.axis_size(name) for name in USERS)

    item_part, user_part = pl.pallas_call(
        lambda *refs: local_kernel(scales, sizes, *refs),
        out_shape=(
            jax.ShapeDtypeStruct((item_rows, feat_width), F32),
            jax.ShapeDtypeStruct((user_rows, feat_width), F32),
        ),
        in_specs=[pl.BlockSpec(memory_space=pltpu.HBM)] * 5,
        out_specs=(
            pl.BlockSpec(memory_space=pltpu.VMEM),
            pl.BlockSpec(memory_space=pltpu.VMEM),
        ),
        scratch_shapes=[
            pltpu.VMEM(user_factors.shape, BF16),
            pltpu.VMEM(item_factors.shape, BF16),
            pltpu.VMEM(confidence.shape, BF16),
            pltpu.SMEM(pattern.shape, jnp.int32),
            pltpu.SMEM((1, user_tiles), jnp.int32),
            pltpu.VMEM((item_tiles, user_rows, tile_rows), F32),
            pltpu.VMEM((item_tiles, user_rows, tile_rows), F32),
            pltpu.SemaphoreType.DMA((5,)),
        ],
        compiler_params=pltpu.CompilerParams(vmem_limit_bytes=60 * 1024 * 1024),
        name="local_sums",
    )(user_factors, item_factors, confidence, pattern, counts.T)

    def reduce_over(part, axes):
        size = lax.axis_size(axes)
        moved = lax.all_to_all(part, axes, 0, 0, tiled=True)
        return moved.reshape(size, part.shape[0] // size, feat_width).sum(0)

    item_half = reduce_over(item_part, ("x", "zl"))
    item_gradient = reduce_over(item_half, "zh")

    user_pair = lax.psum_scatter(user_part, "y", scatter_dimension=0, tiled=True)
    cores = lax.axis_size("core")
    share_rows = user_pair.shape[0] // cores
    core = lax.axis_index("core")
    mine = lax.dynamic_slice_in_dim(user_pair, core * share_rows, share_rows, 0)
    if cores == 1:
        user_gradient = mine
    else:
        other = lax.dynamic_slice_in_dim(user_pair, (1 - core) * share_rows, share_rows, 0)
        user_gradient = mine + lax.ppermute(other, "core", [(0, 1), (1, 0)])
    return (user_gradient, item_gradient[None])


def solution(mesh):
    fine = Mesh(mesh.devices.reshape(4, 8, 2, 8, 2), USERS + ITEMS)
    return jax.shard_map(
        shards,
        mesh=fine,
        in_specs=(
            P(USERS, None),
            P(ITEMS, None),
            P(USERS, ITEMS, None),
            P(USERS, ITEMS),
            P(USERS, ITEMS, None, None, None),
        ),
        out_specs=(P(USERS + ITEMS, None), P(ITEMS, USERS, None)),
        check_vma=False,
    )
```

```python
import math

import jax
import jax.numpy as jnp
from jax import lax
from jax.experimental import pallas as pl
from jax.experimental.pallas import tpu as pltpu
from jax.sharding import Mesh, PartitionSpec as P

WEIGHT_ALL = 8.0
RIDGE_COEF = 0.5
F32 = jnp.float32
BF16 = jnp.bfloat16
USERS = ("x", "zh", "zl")
ITEMS = ("y", "core")


def dot(a, b, dims):
    return lax.dot_general(a, b, (dims, ((), ())), preferred_element_type=F32)


def split(a):
    high = a.astype(BF16)
    return high, (a - high.astype(F32)).astype(BF16)


def eye(n, value):
    row = lax.broadcasted_iota(jnp.int32, (n, n), 0)
    col = lax.broadcasted_iota(jnp.int32, (n, n), 1)
    return jnp.where(row == col, value, 0.0).astype(F32)


def local_kernel(scales, sizes, x_hbm, y_hbm, c_hbm, pat_hbm, cnt_hbm, item_ref, keep_ref, send_ref,
                 x_ref, y_ref, c_ref, pat, cnt, s_ref, w_ref, sems):
    item_scale, item_gram, item_ridge, user_scale, user_gram, user_ridge = scales
    x_size, zh_size, zl_size, y_size, core_size = sizes
    user_tiles, _, slots, tile, _ = c_ref.shape
    width = x_ref.shape[1]
    item_rows = y_ref.shape[0]
    item_tiles = item_rows // tile
    owner_rows = item_rows // (x_size * zh_size * zl_size)
    block = min(tile, owner_rows)
    copies = [
        pltpu.make_async_copy(src, dst, sems.at[k])
        for k, (src, dst) in enumerate(
            ((x_hbm, x_ref), (y_hbm, y_ref), (pat_hbm, pat), (cnt_hbm, cnt), (c_hbm, c_ref)))
    ]
    for copy in copies:
        copy.start()
    w_ref[...] = jnp.zeros_like(w_ref)
    copies[0].wait()
    copies[1].wait()
    x = x_ref[...]
    for t in range(item_tiles):
        s_ref[t] = dot(x, y_ref[t * tile:(t + 1) * tile, :], ((1,), (1,))) - 1.0
    for copy in copies[2:]:
        copy.wait()
    for b in range(user_tiles):
        rows = pl.ds(b * tile, tile)
        for s in range(slots):
            t = pat[b, 0, s]
            live = jnp.where(s < cnt[0, b], 1.0, 0.0).astype(F32)
            residual = (live * c_ref[b, 0, s].astype(F32) * s_ref[t, rows, :]).astype(BF16)
            w_ref[t, rows, :] += residual.astype(F32)
    gx_high, gx_low = split(dot(x, x, ((0,), (0,))) * item_gram + eye(width, item_ridge))
    y = y_ref[...]
    gy_high, gy_low = split(dot(y, y, ((0,), (0,))) * user_gram + eye(width, user_ridge))
    user = jnp.zeros(x_ref.shape, F32)
    for t in range(item_tiles):
        y_t = y_ref[t * tile:(t + 1) * tile, :]
        high, low = split(w_ref[t])
        user += dot(high, y_t, ((1,), (0,))) + dot(low, y_t, ((1,), (0,)))
        part = dot(high, x, ((0,), (0,))) + dot(low, x, ((0,), (0,)))
        gram = dot(y_t, gx_high, ((1,), (0,))) + dot(y_t, gx_low, ((1,), (0,)))
        whole = part * item_scale + gram
        for k in range(0, tile, block):
            owner, offset = divmod(t * tile + k, owner_rows)
            xi, zh, zl = owner // (zh_size * zl_size), owner // zl_size % zh_size, owner % zl_size
            place = ((xi * zl_size + zl) * zh_size + zh) * owner_rows + offset
            item_ref[place:place + block, :] = whole[k:k + block, :]
    gram = dot(x, gy_high, ((1,), (0,))) + dot(x, gy_low, ((1,), (0,)))
    user = user * user_scale + gram
    half = keep_ref.shape[0]
    share = 2 * half // (y_size * core_size)
    my_y, my_core = lax.axis_index("y"), lax.axis_index("core")
    for k in range(y_size * core_size):
        rows = user[k * share:(k + 1) * share, :]
        place = jnp.int32(0)
        bit = half
        for dest, mine, size in ((k % core_size, my_core, core_size), (k // core_size, my_y, y_size)):
            for level in range(size.bit_length() - 1):
                differs = (mine // 2 ** level + dest // 2 ** level) % 2
                if bit == half:
                    away = differs
                else:
                    place += differs * bit
                bit //= 2
        place = pl.multiple_of(place, share)

        @pl.when(away == 0)
        def _():
            keep_ref[pl.ds(place, share), :] = rows

        @pl.when(away == 1)
        def _():
            send_ref[pl.ds(place, share), :] = rows


def shards(user_factors, item_factors, pattern, counts, confidence):
    user_size = lax.axis_size(USERS)
    item_size = lax.axis_size(ITEMS)
    user_rows, feat_width = user_factors.shape
    item_rows = item_factors.shape[0]
    tile_rows = confidence.shape[-1]
    slot_count = pattern.shape[-1]
    user_tiles = user_rows // tile_rows
    item_tiles = item_rows // tile_rows
    users_total = user_rows * user_size
    items_total = item_rows * item_size
    norm_user = math.sqrt(slot_count * item_size * tile_rows)
    norm_item = math.sqrt(users_total * slot_count / item_tiles)
    scales = (
        2.0 / norm_item, 2.0 * WEIGHT_ALL / users_total, 2.0 * RIDGE_COEF / user_size,
        2.0 / norm_user, 2.0 * WEIGHT_ALL / items_total, 2.0 * RIDGE_COEF / item_size,
    )
    sizes = tuple(lax.axis_size(name) for name in USERS + ITEMS)

    item_part, keep, send = pl.pallas_call(
        lambda *refs: local_kernel(scales, sizes, *refs),
        out_shape=(
            jax.ShapeDtypeStruct((item_rows, feat_width), F32),
            jax.ShapeDtypeStruct((user_rows // 2, feat_width), F32),
            jax.ShapeDtypeStruct((user_rows // 2, feat_width), F32),
        ),
        in_specs=[pl.BlockSpec(memory_space=pltpu.HBM)] * 5,
        out_specs=(
            pl.BlockSpec(memory_space=pltpu.VMEM),
            pl.BlockSpec(memory_space=pltpu.VMEM),
            pl.BlockSpec(memory_space=pltpu.VMEM),
        ),
        scratch_shapes=[
            pltpu.VMEM(user_factors.shape, BF16),
            pltpu.VMEM(item_factors.shape, BF16),
            pltpu.VMEM(confidence.shape, BF16),
            pltpu.SMEM(pattern.shape, jnp.int32),
            pltpu.SMEM((1, user_tiles), jnp.int32),
            pltpu.VMEM((item_tiles, user_rows, tile_rows), F32),
            pltpu.VMEM((item_tiles, user_rows, tile_rows), F32),
            pltpu.SemaphoreType.DMA((5,)),
        ],
        compiler_params=pltpu.CompilerParams(vmem_limit_bytes=60 * 1024 * 1024),
        name="local_sums",
    )(user_factors, item_factors, confidence, pattern, counts.T)

    def exchange(part, axes):
        size = lax.axis_size(axes)
        moved = lax.all_to_all(part, axes, 0, 0, tiled=True)
        return moved.reshape(size, part.shape[0] // size, feat_width)

    def halve(keep, send, name, distance):
        pairs = [(i, i ^ distance) for i in range(lax.axis_size(name))]
        whole = keep + lax.ppermute(send, name, pairs)
        half = whole.shape[0] // 2
        return whole[:half], whole[half:], whole

    steps = [(name, 2 ** level) for name in ("core", "y") for level in range(lax.axis_size(name).bit_length() - 1)]
    moved = exchange(item_part, ("x", "zl"))
    for step in steps[:-1]:
        keep, send, _ = halve(keep, send, *step)
    moved, keep, send = lax.optimization_barrier((moved, keep, send))
    item_gradient = exchange(moved.sum(0), "zh").sum(0)
    user_gradient = halve(keep, send, *steps[-1])[2]
    return (user_gradient, item_gradient[None])


def solution(mesh):
    fine = Mesh(mesh.devices.reshape(4, 8, 2, 8, 2), USERS + ITEMS)
    return jax.shard_map(
        shards,
        mesh=fine,
        in_specs=(
            P(USERS, None),
            P(ITEMS, None),
            P(USERS, ITEMS, None),
            P(USERS, ITEMS),
            P(USERS, ITEMS, None, None, None),
        ),
        out_specs=(P(USERS + ITEMS, None), P(ITEMS, USERS, None)),
        check_vma=False,
    )
```

```python
import math

import jax
import jax.numpy as jnp
from jax import lax
from jax.experimental import pallas as pl
from jax.experimental.pallas import tpu as pltpu
from jax.sharding import Mesh, PartitionSpec as P

WEIGHT_ALL = 8.0
RIDGE_COEF = 0.5
F32 = jnp.float32
BF16 = jnp.bfloat16
USERS = ("x", "zh", "zl")
ITEMS = ("y", "core")


def dot(a, b, dims):
    return lax.dot_general(a, b, (dims, ((), ())), preferred_element_type=F32)


def split(a):
    high = a.astype(BF16)
    return high, (a - high.astype(F32)).astype(BF16)


def eye(n, value):
    row = lax.broadcasted_iota(jnp.int32, (n, n), 0)
    col = lax.broadcasted_iota(jnp.int32, (n, n), 1)
    return jnp.where(row == col, value, 0.0).astype(F32)


def item_kernel(scales, sizes, x_hbm, y_hbm, c_hbm, pat_hbm, cnt_hbm, item_hbm, high_hbm, low_hbm,
                x_ref, y_ref, c_ref, pat, cnt, s_ref, w_ref, high_ref, low_ref, item_ref, in_sems, out_sems):
    item_scale, item_gram, item_ridge = scales
    x_size, zh_size, zl_size = sizes
    user_tiles, _, slots, tile, _ = c_ref.shape
    width = x_ref.shape[1]
    item_rows = y_ref.shape[0]
    item_tiles = item_rows // tile
    owner_rows = item_rows // (x_size * zh_size * zl_size)
    block = min(tile, owner_rows)
    parts = 4
    span = item_rows // parts
    moves = [(x_hbm, x_ref), (pat_hbm, pat), (cnt_hbm, cnt)]
    moves += [(y_hbm.at[pl.ds(k * span, span)], y_ref.at[pl.ds(k * span, span)]) for k in range(parts)]
    moves += [(c_hbm.at[b], c_ref.at[b]) for b in range(user_tiles)]
    loads = [pltpu.make_async_copy(src, dst, in_sems.at[k]) for k, (src, dst) in enumerate(moves)]
    for load in loads:
        load.start()
    w_ref[...] = jnp.zeros_like(w_ref)
    loads[0].wait()
    x = x_ref[...]
    gx_high, gx_low = split(dot(x, x, ((0,), (0,))) * item_gram + eye(width, item_ridge))
    for t in range(item_tiles):
        if t * tile % span == 0:
            loads[3 + t * tile // span].wait()
        s_ref[t] = dot(x, y_ref[t * tile:(t + 1) * tile, :], ((1,), (1,))) - 1.0
    loads[1].wait()
    loads[2].wait()
    for b in range(user_tiles):
        loads[3 + parts + b].wait()
        rows = pl.ds(b * tile, tile)
        for s in range(slots):
            t = pat[b, 0, s]
            live = jnp.where(s < cnt[0, b], 1.0, 0.0).astype(F32)
            residual = (live * c_ref[b, 0, s].astype(F32) * s_ref[t, rows, :]).astype(BF16)
            w_ref[t, rows, :] += residual.astype(F32)
    stores = []

    def store(src, dst):
        copy = pltpu.make_async_copy(src, dst, out_sems.at[len(stores)])
        copy.start()
        stores.append(copy)

    for t in range(item_tiles):
        y_t = y_ref[t * tile:(t + 1) * tile, :]
        high, low = split(w_ref[t])
        high_ref[t] = high
        low_ref[t] = low
        part = dot(high, x, ((0,), (0,))) + dot(low, x, ((0,), (0,)))
        gram = dot(y_t, gx_high, ((1,), (0,))) + dot(y_t, gx_low, ((1,), (0,)))
        whole = part * item_scale + gram
        for k in range(0, tile, block):
            owner, offset = divmod(t * tile + k, owner_rows)
            xi, zh, zl = owner // (zh_size * zl_size), owner // zl_size % zh_size, owner % zl_size
            place = ((xi * zl_size + zl) * zh_size + zh) * owner_rows + offset
            item_ref[place:place + block, :] = whole[k:k + block, :]
        if owner_rows < tile:
            count = tile // (owner_rows * zl_size)
            zh = t * tile // (owner_rows * zl_size) % zh_size
            for zl in range(zl_size):
                first = ((xi * zl_size + zl) * zh_size + zh) * owner_rows
                where = pl.ds(first, count * owner_rows)
                store(item_ref.at[where], item_hbm.at[where])
    if owner_rows >= tile:
        store(item_ref, item_hbm)
    store(high_ref, high_hbm)
    store(low_ref, low_hbm)
    for copy in stores:
        copy.wait()


def user_kernel(scales, sizes, x_hbm, y_hbm, high_hbm, low_hbm, keep_ref, send_ref,
                x_ref, y_ref, high_ref, low_ref, in_sems):
    user_scale, user_gram, user_ridge = scales
    y_size, core_size = sizes
    item_tiles, _, tile = high_ref.shape
    width = x_ref.shape[1]
    moves = ((y_hbm, y_ref), (x_hbm, x_ref), (high_hbm, high_ref), (low_hbm, low_ref))
    loads = [pltpu.make_async_copy(src, dst, in_sems.at[k]) for k, (src, dst) in enumerate(moves)]
    for load in loads:
        load.start()
    loads[0].wait()
    y = y_ref[...]
    gy_high, gy_low = split(dot(y, y, ((0,), (0,))) * user_gram + eye(width, user_ridge))
    for load in loads[1:]:
        load.wait()
    x = x_ref[...]
    user = jnp.zeros(x_ref.shape, F32)
    for t in range(item_tiles):
        y_t = y_ref[t * tile:(t + 1) * tile, :]
        user += dot(high_ref[t], y_t, ((1,), (0,))) + dot(low_ref[t], y_t, ((1,), (0,)))
    gram = dot(x, gy_high, ((1,), (0,))) + dot(x, gy_low, ((1,), (0,)))
    user = user * user_scale + gram
    half = keep_ref.shape[0]
    share = 2 * half // (y_size * core_size)
    my_y, my_core = lax.axis_index("y"), lax.axis_index("core")
    for k in range(y_size * core_size):
        rows = user[k * share:(k + 1) * share, :]
        place = jnp.int32(0)
        bit = half
        for dest, mine, size in ((k % core_size, my_core, core_size), (k // core_size, my_y, y_size)):
            for level in range(size.bit_length() - 1):
                differs = (mine // 2 ** level + dest // 2 ** level) % 2
                if bit == half:
                    away = differs
                else:
                    place += differs * bit
                bit //= 2
        place = pl.multiple_of(place, share)

        @pl.when(away == 0)
        def _():
            keep_ref[pl.ds(place, share), :] = rows

        @pl.when(away == 1)
        def _():
            send_ref[pl.ds(place, share), :] = rows


def shards(user_factors, item_factors, pattern, counts, confidence):
    user_size = lax.axis_size(USERS)
    item_size = lax.axis_size(ITEMS)
    user_rows, feat_width = user_factors.shape
    item_rows = item_factors.shape[0]
    tile_rows = confidence.shape[-1]
    slot_count = pattern.shape[-1]
    user_tiles = user_rows // tile_rows
    item_tiles = item_rows // tile_rows
    users_total = user_rows * user_size
    items_total = item_rows * item_size
    norm_user = math.sqrt(slot_count * item_size * tile_rows)
    norm_item = math.sqrt(users_total * slot_count / item_tiles)
    item_scales = (2.0 / norm_item, 2.0 * WEIGHT_ALL / users_total, 2.0 * RIDGE_COEF / user_size)
    user_scales = (2.0 / norm_user, 2.0 * WEIGHT_ALL / items_total, 2.0 * RIDGE_COEF / item_size)
    user_axes = tuple(lax.axis_size(name) for name in USERS)
    item_axes = tuple(lax.axis_size(name) for name in ITEMS)
    in_hbm = pl.BlockSpec(memory_space=pltpu.HBM)
    in_vmem = pl.BlockSpec(memory_space=pltpu.VMEM)
    params = pltpu.CompilerParams(vmem_limit_bytes=32 * 1024 * 1024)
    sums_shape = (item_tiles, user_rows, tile_rows)

    def pinned(*arrays):
        return [pltpu.with_memory_space_constraint(a, pltpu.HBM) for a in arrays]

    item_part, high, low = pl.pallas_call(
        lambda *refs: item_kernel(item_scales, user_axes, *refs),
        out_shape=(
            pltpu.HBM((item_rows, feat_width), F32),
            pltpu.HBM(sums_shape, BF16),
            pltpu.HBM(sums_shape, BF16),
        ),
        in_specs=[in_hbm] * 5,
        out_specs=(in_hbm,) * 3,
        scratch_shapes=[
            pltpu.VMEM(user_factors.shape, BF16),
            pltpu.VMEM(item_factors.shape, BF16),
            pltpu.VMEM(confidence.shape, BF16),
            pltpu.SMEM(pattern.shape, jnp.int32),
            pltpu.SMEM((1, user_tiles), jnp.int32),
            pltpu.VMEM(sums_shape, F32),
            pltpu.VMEM(sums_shape, F32),
            pltpu.VMEM(sums_shape, BF16),
            pltpu.VMEM(sums_shape, BF16),
            pltpu.VMEM((item_rows, feat_width), F32),
            pltpu.SemaphoreType.DMA((7 + user_tiles,)),
            pltpu.SemaphoreType.DMA((2 + 2 * item_tiles,)),
        ],
        compiler_params=params,
        name="item_sums",
    )(*pinned(user_factors, item_factors, confidence, pattern, counts.T))

    keep, send = pl.pallas_call(
        lambda *refs: user_kernel(user_scales, item_axes, *refs),
        out_shape=(pltpu.VMEM((user_rows // 2, feat_width), F32),) * 2,
        in_specs=[in_hbm] * 4,
        out_specs=(in_vmem,) * 2,
        scratch_shapes=[
            pltpu.VMEM(user_factors.shape, BF16),
            pltpu.VMEM(item_factors.shape, BF16),
            pltpu.VMEM(sums_shape, BF16),
            pltpu.VMEM(sums_shape, BF16),
            pltpu.SemaphoreType.DMA((4,)),
        ],
        compiler_params=params,
        name="user_sums",
    )(*pinned(user_factors, item_factors, high, low))

    def exchange(part, axes):
        size = lax.axis_size(axes)
        moved = lax.all_to_all(part, axes, 0, 0, tiled=True)
        return moved.reshape(size, part.shape[0] // size, feat_width)

    def halve(keep, send, name, distance):
        pairs = [(i, i ^ distance) for i in range(lax.axis_size(name))]
        whole = keep + lax.ppermute(send, name, pairs)
        half = whole.shape[0] // 2
        return whole[:half], whole[half:], whole

    steps = [(name, 2 ** level) for name in ("core", "y") for level in range(lax.axis_size(name).bit_length() - 1)]
    moved = exchange(item_part, ("x", "zl"))
    for step in steps[:-1]:
        keep, send, _ = halve(keep, send, *step)
    moved, keep, send = lax.optimization_barrier((moved, keep, send))
    item_gradient = exchange(moved.sum(0), "zh").sum(0)
    user_gradient = halve(keep, send, *steps[-1])[2]
    return (user_gradient, item_gradient[None])


def solution(mesh):
    fine = Mesh(mesh.devices.reshape(4, 8, 2, 8, 2), USERS + ITEMS)
    return jax.shard_map(
        shards,
        mesh=fine,
        in_specs=(
            P(USERS, None),
            P(ITEMS, None),
            P(USERS, ITEMS, None),
            P(USERS, ITEMS),
            P(USERS, ITEMS, None, None, None),
        ),
        out_specs=(P(USERS + ITEMS, None), P(ITEMS, USERS, None)),
        check_vma=False,
    )
```

```python
import math

import jax
import jax.numpy as jnp
from jax import lax
from jax.experimental import pallas as pl
from jax.experimental.pallas import tpu as pltpu
from jax.sharding import Mesh, PartitionSpec as P

WEIGHT_ALL = 8.0
RIDGE_COEF = 0.5
F32 = jnp.float32
BF16 = jnp.bfloat16
USERS = ("x", "zh", "zl")
ITEMS = ("y", "core")


def dot(a, b, dims):
    return lax.dot_general(a, b, (dims, ((), ())), preferred_element_type=F32)


def split(a):
    high = a.astype(BF16)
    return high, (a - high.astype(F32)).astype(BF16)


def eye(n, value):
    row = lax.broadcasted_iota(jnp.int32, (n, n), 0)
    col = lax.broadcasted_iota(jnp.int32, (n, n), 1)
    return jnp.where(row == col, value, 0.0).astype(F32)


def item_kernel(scales, sizes, x_hbm, y_hbm, c_hbm, pat_hbm, cnt_hbm, item_hbm, high_ref, low_ref,
                x_ref, y_ref, c_ref, pat, cnt, s_ref, w_ref, item_ref, in_sems, out_sems):
    item_scale, item_gram, item_ridge = scales
    x_size, zh_size, zl_size = sizes
    user_tiles, _, slots, tile, _ = c_ref.shape
    width = x_ref.shape[1]
    item_rows = y_ref.shape[0]
    item_tiles = item_rows // tile
    owner_rows = item_rows // (x_size * zh_size * zl_size)
    block = min(tile, owner_rows)
    moves = [(x_hbm, x_ref), (pat_hbm, pat), (cnt_hbm, cnt), (y_hbm, y_ref)]
    moves += [(c_hbm.at[b], c_ref.at[b]) for b in range(user_tiles)]
    loads = [pltpu.make_async_copy(src, dst, in_sems.at[k]) for k, (src, dst) in enumerate(moves)]
    for load in loads:
        load.start()
    w_ref[...] = jnp.zeros_like(w_ref)
    loads[0].wait()
    x = x_ref[...]
    gx_high, gx_low = split(dot(x, x, ((0,), (0,))) * item_gram + eye(width, item_ridge))
    loads[3].wait()
    for t in range(item_tiles):
        s_ref[t] = dot(x, y_ref[t * tile:(t + 1) * tile, :], ((1,), (1,))) - 1.0
    loads[1].wait()
    loads[2].wait()
    for b in range(user_tiles):
        loads[4 + b].wait()
        rows = pl.ds(b * tile, tile)
        for s in range(slots):
            t = pat[b, 0, s]
            live = jnp.where(s < cnt[0, b], 1.0, 0.0).astype(F32)
            residual = (live * c_ref[b, 0, s].astype(F32) * s_ref[t, rows, :]).astype(BF16)
            w_ref[t, rows, :] += residual.astype(F32)
    stores = []

    def store(src, dst):
        copy = pltpu.make_async_copy(src, dst, out_sems.at[len(stores)])
        copy.start()
        stores.append(copy)

    for t in range(item_tiles):
        y_t = y_ref[t * tile:(t + 1) * tile, :]
        high, low = split(w_ref[t])
        high_ref[t] = high
        low_ref[t] = low
        part = dot(high, x, ((0,), (0,))) + dot(low, x, ((0,), (0,)))
        gram = dot(y_t, gx_high, ((1,), (0,))) + dot(y_t, gx_low, ((1,), (0,)))
        whole = part * item_scale + gram
        for k in range(0, tile, block):
            owner, offset = divmod(t * tile + k, owner_rows)
            xi, zh, zl = owner // (zh_size * zl_size), owner // zl_size % zh_size, owner % zl_size
            place = ((xi * zl_size + zl) * zh_size + zh) * owner_rows + offset
            item_ref[place:place + block, :] = whole[k:k + block, :]
        if owner_rows < tile:
            count = tile // (owner_rows * zl_size)
            zh = t * tile // (owner_rows * zl_size) % zh_size
            for zl in range(zl_size):
                first = ((xi * zl_size + zl) * zh_size + zh) * owner_rows
                where = pl.ds(first, count * owner_rows)
                store(item_ref.at[where], item_hbm.at[where])
    if owner_rows >= tile:
        store(item_ref, item_hbm)
    for copy in stores:
        copy.wait()


def user_kernel(scales, sizes, x_hbm, y_hbm, high_ref, low_ref, keep_ref, send_ref,
                x_ref, y_ref, in_sems):
    user_scale, user_gram, user_ridge = scales
    y_size, core_size = sizes
    item_tiles, _, tile = high_ref.shape
    width = x_ref.shape[1]
    moves = ((y_hbm, y_ref), (x_hbm, x_ref))
    loads = [pltpu.make_async_copy(src, dst, in_sems.at[k]) for k, (src, dst) in enumerate(moves)]
    for load in loads:
        load.start()
    loads[0].wait()
    y = y_ref[...]
    gy_high, gy_low = split(dot(y, y, ((0,), (0,))) * user_gram + eye(width, user_ridge))
    for load in loads[1:]:
        load.wait()
    x = x_ref[...]
    user = jnp.zeros(x_ref.shape, F32)
    for t in range(item_tiles):
        y_t = y_ref[t * tile:(t + 1) * tile, :]
        user += dot(high_ref[t], y_t, ((1,), (0,))) + dot(low_ref[t], y_t, ((1,), (0,)))
    gram = dot(x, gy_high, ((1,), (0,))) + dot(x, gy_low, ((1,), (0,)))
    user = user * user_scale + gram
    half = keep_ref.shape[0]
    share = 2 * half // (y_size * core_size)
    my_y, my_core = lax.axis_index("y"), lax.axis_index("core")
    for k in range(y_size * core_size):
        rows = user[k * share:(k + 1) * share, :]
        place = jnp.int32(0)
        bit = half
        for dest, mine, size in ((k % core_size, my_core, core_size), (k // core_size, my_y, y_size)):
            for level in range(size.bit_length() - 1):
                differs = (mine // 2 ** level + dest // 2 ** level) % 2
                if bit == half:
                    away = differs
                else:
                    place += differs * bit
                bit //= 2
        place = pl.multiple_of(place, share)

        @pl.when(away == 0)
        def _():
            keep_ref[pl.ds(place, share), :] = rows

        @pl.when(away == 1)
        def _():
            send_ref[pl.ds(place, share), :] = rows


def shards(user_factors, item_factors, pattern, counts, confidence):
    user_size = lax.axis_size(USERS)
    item_size = lax.axis_size(ITEMS)
    user_rows, feat_width = user_factors.shape
    item_rows = item_factors.shape[0]
    tile_rows = confidence.shape[-1]
    slot_count = pattern.shape[-1]
    user_tiles = user_rows // tile_rows
    item_tiles = item_rows // tile_rows
    users_total = user_rows * user_size
    items_total = item_rows * item_size
    norm_user = math.sqrt(slot_count * item_size * tile_rows)
    norm_item = math.sqrt(users_total * slot_count / item_tiles)
    item_scales = (2.0 / norm_item, 2.0 * WEIGHT_ALL / users_total, 2.0 * RIDGE_COEF / user_size)
    user_scales = (2.0 / norm_user, 2.0 * WEIGHT_ALL / items_total, 2.0 * RIDGE_COEF / item_size)
    user_axes = tuple(lax.axis_size(name) for name in USERS)
    item_axes = tuple(lax.axis_size(name) for name in ITEMS)
    in_hbm = pl.BlockSpec(memory_space=pltpu.HBM)
    in_vmem = pl.BlockSpec(memory_space=pltpu.VMEM)
    params = pltpu.CompilerParams(vmem_limit_bytes=32 * 1024 * 1024)
    sums_shape = (item_tiles, user_rows, tile_rows)

    def pinned(*arrays):
        return [pltpu.with_memory_space_constraint(a, pltpu.HBM) for a in arrays]

    item_part, high, low = pl.pallas_call(
        lambda *refs: item_kernel(item_scales, user_axes, *refs),
        out_shape=(
            pltpu.HBM((item_rows, feat_width), F32),
            pltpu.VMEM(sums_shape, BF16),
            pltpu.VMEM(sums_shape, BF16),
        ),
        in_specs=[in_hbm] * 5,
        out_specs=(in_hbm, in_vmem, in_vmem),
        scratch_shapes=[
            pltpu.VMEM(user_factors.shape, BF16),
            pltpu.VMEM(item_factors.shape, BF16),
            pltpu.VMEM(confidence.shape, BF16),
            pltpu.SMEM(pattern.shape, jnp.int32),
            pltpu.SMEM((1, user_tiles), jnp.int32),
            pltpu.VMEM(sums_shape, F32),
            pltpu.VMEM(sums_shape, F32),
            pltpu.VMEM((item_rows, feat_width), F32),
            pltpu.SemaphoreType.DMA((4 + user_tiles,)),
            pltpu.SemaphoreType.DMA((2 * item_tiles,)),
        ],
        compiler_params=params,
        name="item_sums",
    )(*pinned(user_factors, item_factors, confidence, pattern, counts.T))

    keep, send = pl.pallas_call(
        lambda *refs: user_kernel(user_scales, item_axes, *refs),
        out_shape=(pltpu.VMEM((user_rows // 2, feat_width), F32),) * 2,
        in_specs=[in_hbm, in_hbm, in_vmem, in_vmem],
        out_specs=(in_vmem,) * 2,
        scratch_shapes=[
            pltpu.VMEM(user_factors.shape, BF16),
            pltpu.VMEM(item_factors.shape, BF16),
            pltpu.SemaphoreType.DMA((2,)),
        ],
        compiler_params=params,
        name="user_sums",
    )(*pinned(user_factors, item_factors), high, low)

    def exchange(part, axes):
        size = lax.axis_size(axes)
        moved = lax.all_to_all(part, axes, 0, 0, tiled=True)
        return moved.reshape(size, part.shape[0] // size, feat_width)

    def halve(keep, send, name, distance):
        pairs = [(i, i ^ distance) for i in range(lax.axis_size(name))]
        whole = keep + lax.ppermute(send, name, pairs)
        half = whole.shape[0] // 2
        return whole[:half], whole[half:], whole

    steps = [(name, 2 ** level) for name in ("core", "y") for level in range(lax.axis_size(name).bit_length() - 1)]
    moved = exchange(item_part, ("x", "zl"))
    for step in steps[:-1]:
        keep, send, _ = halve(keep, send, *step)
    moved, keep, send = lax.optimization_barrier((moved, keep, send))
    item_gradient = exchange(moved.sum(0), "zh").sum(0)
    user_gradient = halve(keep, send, *steps[-1])[2]
    return (user_gradient, item_gradient[None])


def solution(mesh):
    fine = Mesh(mesh.devices.reshape(4, 8, 2, 8, 2), USERS + ITEMS)
    return jax.shard_map(
        shards,
        mesh=fine,
        in_specs=(
            P(USERS, None),
            P(ITEMS, None),
            P(USERS, ITEMS, None),
            P(USERS, ITEMS),
            P(USERS, ITEMS, None, None, None),
        ),
        out_specs=(P(USERS + ITEMS, None), P(ITEMS, USERS, None)),
        check_vma=False,
    )
```

```python
import math

import jax
import jax.numpy as jnp
from jax import lax
from jax.experimental import pallas as pl
from jax.experimental.pallas import tpu as pltpu
from jax.sharding import Mesh, PartitionSpec as P

WEIGHT_ALL = 8.0
RIDGE_COEF = 0.5
F32 = jnp.float32
BF16 = jnp.bfloat16
USERS = ("x", "zh", "zl")
ITEMS = ("y", "core")


def dot(a, b, dims):
    return lax.dot_general(a, b, (dims, ((), ())), preferred_element_type=F32)


def split(a):
    high = a.astype(BF16)
    return high, (a - high.astype(F32)).astype(BF16)


def eye(n, value):
    row = lax.broadcasted_iota(jnp.int32, (n, n), 0)
    col = lax.broadcasted_iota(jnp.int32, (n, n), 1)
    return jnp.where(row == col, value, 0.0).astype(F32)


def residual_sums(x_hbm, y_hbm, c_hbm, pat_hbm, cnt_hbm, x_ref, y_ref, c_ref, pat, cnt, s_ref, w_ref, sems, during):
    user_tiles, _, slots, tile, _ = c_ref.shape
    moves = [(x_hbm, x_ref), (pat_hbm, pat), (cnt_hbm, cnt), (y_hbm, y_ref)]
    moves += [(c_hbm.at[b], c_ref.at[b]) for b in range(user_tiles)]
    loads = [pltpu.make_async_copy(src, dst, sems.at[k]) for k, (src, dst) in enumerate(moves)]
    for load in loads:
        load.start()
    w_ref[...] = jnp.zeros_like(w_ref)
    loads[0].wait()
    x = x_ref[...]
    early = during(x)
    loads[3].wait()
    for t in range(w_ref.shape[0]):
        s_ref[t] = dot(x, y_ref[t * tile:(t + 1) * tile, :], ((1,), (1,))) - 1.0
    loads[1].wait()
    loads[2].wait()
    for b in range(user_tiles):
        loads[4 + b].wait()
        rows = pl.ds(b * tile, tile)
        for s in range(slots):
            t = pat[b, 0, s]
            live = jnp.where(s < cnt[0, b], 1.0, 0.0).astype(F32)
            residual = (live * c_ref[b, 0, s].astype(F32) * s_ref[t, rows, :]).astype(BF16)
            w_ref[t, rows, :] += residual.astype(F32)
    return early


def item_kernel(scales, sizes, x_hbm, y_hbm, c_hbm, pat_hbm, cnt_hbm, item_hbm,
                x_ref, y_ref, c_ref, pat, cnt, s_ref, w_ref, in_sems, item_ref, out_sems):
    item_scale, item_gram, item_ridge = scales
    x_size, zh_size, zl_size = sizes
    tile = c_ref.shape[-1]
    width = x_ref.shape[1]
    item_rows = y_ref.shape[0]
    item_tiles = item_rows // tile
    owner_rows = item_rows // (x_size * zh_size * zl_size)
    block = min(tile, owner_rows)

    def own_gram(x):
        return split(dot(x, x, ((0,), (0,))) * item_gram + eye(width, item_ridge))

    gx_high, gx_low = residual_sums(
        x_hbm, y_hbm, c_hbm, pat_hbm, cnt_hbm, x_ref, y_ref, c_ref, pat, cnt, s_ref, w_ref, in_sems, own_gram)
    x = x_ref[...]
    stores = []

    def store(src, dst):
        copy = pltpu.make_async_copy(src, dst, out_sems.at[len(stores)])
        copy.start()
        stores.append(copy)

    for t in range(item_tiles):
        y_t = y_ref[t * tile:(t + 1) * tile, :]
        high, low = split(w_ref[t])
        part = dot(high, x, ((0,), (0,))) + dot(low, x, ((0,), (0,)))
        gram = dot(y_t, gx_high, ((1,), (0,))) + dot(y_t, gx_low, ((1,), (0,)))
        whole = part * item_scale + gram
        for k in range(0, tile, block):
            owner, offset = divmod(t * tile + k, owner_rows)
            xi, zh, zl = owner // (zh_size * zl_size), owner // zl_size % zh_size, owner % zl_size
            place = ((xi * zl_size + zl) * zh_size + zh) * owner_rows + offset
            item_ref[place:place + block, :] = whole[k:k + block, :]
        if owner_rows < tile:
            count = tile // (owner_rows * zl_size)
            zh = t * tile // (owner_rows * zl_size) % zh_size
            for zl in range(zl_size):
                first = ((xi * zl_size + zl) * zh_size + zh) * owner_rows
                where = pl.ds(first, count * owner_rows)
                store(item_ref.at[where], item_hbm.at[where])
    if owner_rows >= tile:
        store(item_ref, item_hbm)
    for copy in stores:
        copy.wait()


def user_kernel(scales, sizes, x_hbm, y_hbm, c_hbm, pat_hbm, cnt_hbm, keep_ref, send_ref,
                x_ref, y_ref, c_ref, pat, cnt, s_ref, w_ref, in_sems):
    user_scale, user_gram, user_ridge = scales
    y_size, core_size = sizes
    tile = c_ref.shape[-1]
    width = x_ref.shape[1]
    residual_sums(
        x_hbm, y_hbm, c_hbm, pat_hbm, cnt_hbm, x_ref, y_ref, c_ref, pat, cnt, s_ref, w_ref, in_sems, lambda x: None)
    x = x_ref[...]
    y = y_ref[...]
    gy_high, gy_low = split(dot(y, y, ((0,), (0,))) * user_gram + eye(width, user_ridge))
    user = jnp.zeros(x_ref.shape, F32)
    for t in range(w_ref.shape[0]):
        y_t = y_ref[t * tile:(t + 1) * tile, :]
        high, low = split(w_ref[t])
        user += dot(high, y_t, ((1,), (0,))) + dot(low, y_t, ((1,), (0,)))
    gram = dot(x, gy_high, ((1,), (0,))) + dot(x, gy_low, ((1,), (0,)))
    user = user * user_scale + gram
    half = keep_ref.shape[0]
    share = 2 * half // (y_size * core_size)
    my_y, my_core = lax.axis_index("y"), lax.axis_index("core")
    for k in range(y_size * core_size):
        rows = user[k * share:(k + 1) * share, :]
        place = jnp.int32(0)
        bit = half
        for dest, mine, size in ((k % core_size, my_core, core_size), (k // core_size, my_y, y_size)):
            for level in range(size.bit_length() - 1):
                differs = (mine // 2 ** level + dest // 2 ** level) % 2
                if bit == half:
                    away = differs
                else:
                    place += differs * bit
                bit //= 2
        place = pl.multiple_of(place, share)

        @pl.when(away == 0)
        def _():
            keep_ref[pl.ds(place, share), :] = rows

        @pl.when(away == 1)
        def _():
            send_ref[pl.ds(place, share), :] = rows


def shards(user_factors, item_factors, pattern, counts, confidence):
    user_size = lax.axis_size(USERS)
    item_size = lax.axis_size(ITEMS)
    user_rows, feat_width = user_factors.shape
    item_rows = item_factors.shape[0]
    tile_rows = confidence.shape[-1]
    slot_count = pattern.shape[-1]
    user_tiles = user_rows // tile_rows
    item_tiles = item_rows // tile_rows
    users_total = user_rows * user_size
    items_total = item_rows * item_size
    norm_user = math.sqrt(slot_count * item_size * tile_rows)
    norm_item = math.sqrt(users_total * slot_count / item_tiles)
    item_scales = (2.0 / norm_item, 2.0 * WEIGHT_ALL / users_total, 2.0 * RIDGE_COEF / user_size)
    user_scales = (2.0 / norm_user, 2.0 * WEIGHT_ALL / items_total, 2.0 * RIDGE_COEF / item_size)
    user_axes = tuple(lax.axis_size(name) for name in USERS)
    item_axes = tuple(lax.axis_size(name) for name in ITEMS)
    in_hbm = pl.BlockSpec(memory_space=pltpu.HBM)
    in_vmem = pl.BlockSpec(memory_space=pltpu.VMEM)
    params = pltpu.CompilerParams(vmem_limit_bytes=32 * 1024 * 1024)
    sums_shape = (item_tiles, user_rows, tile_rows)

    def pinned(*arrays):
        return [pltpu.with_memory_space_constraint(a, pltpu.HBM) for a in arrays]

    operands = pinned(user_factors, item_factors, confidence, pattern, counts.T)
    scratch = [
        pltpu.VMEM(user_factors.shape, BF16),
        pltpu.VMEM(item_factors.shape, BF16),
        pltpu.VMEM(confidence.shape, BF16),
        pltpu.SMEM(pattern.shape, jnp.int32),
        pltpu.SMEM((1, user_tiles), jnp.int32),
        pltpu.VMEM(sums_shape, F32),
        pltpu.VMEM(sums_shape, F32),
        pltpu.SemaphoreType.DMA((4 + user_tiles,)),
    ]

    item_part = pl.pallas_call(
        lambda *refs: item_kernel(item_scales, user_axes, *refs),
        out_shape=pltpu.HBM((item_rows, feat_width), F32),
        in_specs=[in_hbm] * 5,
        out_specs=in_hbm,
        scratch_shapes=scratch + [
            pltpu.VMEM((item_rows, feat_width), F32),
            pltpu.SemaphoreType.DMA((2 * item_tiles,)),
        ],
        compiler_params=params,
        name="item_sums",
    )(*operands)

    keep, send = pl.pallas_call(
        lambda *refs: user_kernel(user_scales, item_axes, *refs),
        out_shape=(pltpu.VMEM((user_rows // 2, feat_width), F32),) * 2,
        in_specs=[in_hbm] * 5,
        out_specs=(in_vmem,) * 2,
        scratch_shapes=scratch,
        compiler_params=params,
        name="user_sums",
    )(*operands)

    def exchange(part, axes):
        size = lax.axis_size(axes)
        moved = lax.all_to_all(part, axes, 0, 0, tiled=True)
        return moved.reshape(size, part.shape[0] // size, feat_width)

    def halve(keep, send, name, distance):
        pairs = [(i, i ^ distance) for i in range(lax.axis_size(name))]
        whole = keep + lax.ppermute(send, name, pairs)
        half = whole.shape[0] // 2
        return whole[:half], whole[half:], whole

    steps = [(name, 2 ** level) for name in ("core", "y") for level in range(lax.axis_size(name).bit_length() - 1)]
    moved = exchange(item_part, ("x", "zl"))
    for step in steps[:-1]:
        keep, send, _ = halve(keep, send, *step)
    moved, keep, send = lax.optimization_barrier((moved, keep, send))
    item_gradient = exchange(moved.sum(0), "zh").sum(0)
    user_gradient = halve(keep, send, *steps[-1])[2]
    return (user_gradient, item_gradient[None])


def solution(mesh):
    fine = Mesh(mesh.devices.reshape(4, 8, 2, 8, 2), USERS + ITEMS)
    return jax.shard_map(
        shards,
        mesh=fine,
        in_specs=(
            P(USERS, None),
            P(ITEMS, None),
            P(USERS, ITEMS, None),
            P(USERS, ITEMS),
            P(USERS, ITEMS, None, None, None),
        ),
        out_specs=(P(USERS + ITEMS, None), P(ITEMS, USERS, None)),
        check_vma=False,
    )
```

```python
import math

import jax
import jax.numpy as jnp
from jax import lax
from jax.experimental import pallas as pl
from jax.experimental.pallas import tpu as pltpu
from jax.sharding import Mesh, PartitionSpec as P

WEIGHT_ALL = 8.0
RIDGE_COEF = 0.5
F32 = jnp.float32
BF16 = jnp.bfloat16
USERS = ("x", "zh", "zl")
ITEMS = ("y", "core")


def dot(a, b, dims):
    return lax.dot_general(a, b, (dims, ((), ())), preferred_element_type=F32)


def split(a):
    high = a.astype(BF16)
    return high, (a - high.astype(F32)).astype(BF16)


def eye(n, value):
    row = lax.broadcasted_iota(jnp.int32, (n, n), 0)
    col = lax.broadcasted_iota(jnp.int32, (n, n), 1)
    return jnp.where(row == col, value, 0.0).astype(F32)


def residual_sums(x_hbm, y_hbm, c_hbm, pat_hbm, cnt_hbm, x_ref, y_ref, c_ref, pat, cnt, s_ref, w_ref, sems, during):
    user_tiles, _, slots, tile, _ = c_ref.shape
    moves = [(x_hbm, x_ref), (pat_hbm, pat), (cnt_hbm, cnt), (y_hbm, y_ref)]
    moves += [(c_hbm.at[b], c_ref.at[b]) for b in range(user_tiles)]
    loads = [pltpu.make_async_copy(src, dst, sems.at[k]) for k, (src, dst) in enumerate(moves)]
    for load in loads:
        load.start()
    w_ref[...] = jnp.zeros_like(w_ref)
    loads[0].wait()
    x = x_ref[...]
    early = during(x)
    loads[3].wait()
    for t in range(0, w_ref.shape[0], 2):
        pair = dot(x, y_ref[t * tile:(t + 2) * tile, :], ((1,), (1,))) - 1.0
        s_ref[t] = pair[:, :tile]
        s_ref[t + 1] = pair[:, tile:]
    loads[1].wait()
    loads[2].wait()
    for b in range(user_tiles):
        loads[4 + b].wait()
        rows = pl.ds(b * tile, tile)
        for s in range(slots):
            t = pat[b, 0, s]
            live = jnp.where(s < cnt[0, b], 1.0, 0.0).astype(F32)
            residual = (live * c_ref[b, 0, s].astype(F32) * s_ref[t, rows, :]).astype(BF16)
            w_ref[t, rows, :] += residual.astype(F32)
    return early


def item_kernel(scales, sizes, x_hbm, y_hbm, c_hbm, pat_hbm, cnt_hbm, item_hbm,
                x_ref, y_ref, c_ref, pat, cnt, s_ref, w_ref, in_sems, item_ref, out_sems):
    item_scale, item_gram, item_ridge = scales
    x_size, zh_size, zl_size = sizes
    tile = c_ref.shape[-1]
    width = x_ref.shape[1]
    item_rows = y_ref.shape[0]
    item_tiles = item_rows // tile
    owner_rows = item_rows // (x_size * zh_size * zl_size)
    block = min(tile, owner_rows)

    def own_gram(x):
        return split(dot(x, x, ((0,), (0,))) * item_gram + eye(width, item_ridge))

    gx_high, gx_low = residual_sums(
        x_hbm, y_hbm, c_hbm, pat_hbm, cnt_hbm, x_ref, y_ref, c_ref, pat, cnt, s_ref, w_ref, in_sems, own_gram)
    x = x_ref[...]
    stores = []

    def store(src, dst):
        copy = pltpu.make_async_copy(src, dst, out_sems.at[len(stores)])
        copy.start()
        stores.append(copy)

    for t in range(item_tiles):
        y_t = y_ref[t * tile:(t + 1) * tile, :]
        high, low = split(w_ref[t])
        part = dot(high, x, ((0,), (0,))) + dot(low, x, ((0,), (0,)))
        gram = dot(y_t, gx_high, ((1,), (0,))) + dot(y_t, gx_low, ((1,), (0,)))
        whole = part * item_scale + gram
        for k in range(0, tile, block):
            owner, offset = divmod(t * tile + k, owner_rows)
            xi, zh, zl = owner // (zh_size * zl_size), owner // zl_size % zh_size, owner % zl_size
            place = ((xi * zl_size + zl) * zh_size + zh) * owner_rows + offset
            item_ref[place:place + block, :] = whole[k:k + block, :]
        if owner_rows < tile:
            count = tile // (owner_rows * zl_size)
            zh = t * tile // (owner_rows * zl_size) % zh_size
            for zl in range(zl_size):
                first = ((xi * zl_size + zl) * zh_size + zh) * owner_rows
                where = pl.ds(first, count * owner_rows)
                store(item_ref.at[where], item_hbm.at[where])
    if owner_rows >= tile:
        store(item_ref, item_hbm)
    for copy in stores:
        copy.wait()


def user_kernel(scales, sizes, x_hbm, y_hbm, c_hbm, pat_hbm, cnt_hbm, keep_ref, send_ref,
                x_ref, y_ref, c_ref, pat, cnt, s_ref, w_ref, in_sems):
    user_scale, user_gram, user_ridge = scales
    y_size, core_size = sizes
    tile = c_ref.shape[-1]
    width = x_ref.shape[1]
    residual_sums(
        x_hbm, y_hbm, c_hbm, pat_hbm, cnt_hbm, x_ref, y_ref, c_ref, pat, cnt, s_ref, w_ref, in_sems, lambda x: None)
    x = x_ref[...]
    y = y_ref[...]
    gy_high, gy_low = split(dot(y, y, ((0,), (0,))) * user_gram + eye(width, user_ridge))
    user = jnp.zeros(x_ref.shape, F32)
    for t in range(w_ref.shape[0]):
        y_t = y_ref[t * tile:(t + 1) * tile, :]
        high, low = split(w_ref[t])
        user += dot(high, y_t, ((1,), (0,))) + dot(low, y_t, ((1,), (0,)))
    gram = dot(x, gy_high, ((1,), (0,))) + dot(x, gy_low, ((1,), (0,)))
    user = user * user_scale + gram
    half = keep_ref.shape[0]
    share = 2 * half // (y_size * core_size)
    my_y, my_core = lax.axis_index("y"), lax.axis_index("core")
    for k in range(y_size * core_size):
        rows = user[k * share:(k + 1) * share, :]
        place = jnp.int32(0)
        bit = half
        for dest, mine, size in ((k % core_size, my_core, core_size), (k // core_size, my_y, y_size)):
            for level in range(size.bit_length() - 1):
                differs = (mine // 2 ** level + dest // 2 ** level) % 2
                if bit == half:
                    away = differs
                else:
                    place += differs * bit
                bit //= 2
        place = pl.multiple_of(place, share)

        @pl.when(away == 0)
        def _():
            keep_ref[pl.ds(place, share), :] = rows

        @pl.when(away == 1)
        def _():
            send_ref[pl.ds(place, share), :] = rows


def shards(user_factors, item_factors, pattern, counts, confidence):
    user_size = lax.axis_size(USERS)
    item_size = lax.axis_size(ITEMS)
    user_rows, feat_width = user_factors.shape
    item_rows = item_factors.shape[0]
    tile_rows = confidence.shape[-1]
    slot_count = pattern.shape[-1]
    user_tiles = user_rows // tile_rows
    item_tiles = item_rows // tile_rows
    users_total = user_rows * user_size
    items_total = item_rows * item_size
    norm_user = math.sqrt(slot_count * item_size * tile_rows)
    norm_item = math.sqrt(users_total * slot_count / item_tiles)
    item_scales = (2.0 / norm_item, 2.0 * WEIGHT_ALL / users_total, 2.0 * RIDGE_COEF / user_size)
    user_scales = (2.0 / norm_user, 2.0 * WEIGHT_ALL / items_total, 2.0 * RIDGE_COEF / item_size)
    user_axes = tuple(lax.axis_size(name) for name in USERS)
    item_axes = tuple(lax.axis_size(name) for name in ITEMS)
    in_hbm = pl.BlockSpec(memory_space=pltpu.HBM)
    in_vmem = pl.BlockSpec(memory_space=pltpu.VMEM)
    params = pltpu.CompilerParams(vmem_limit_bytes=32 * 1024 * 1024)
    sums_shape = (item_tiles, user_rows, tile_rows)

    def pinned(*arrays):
        return [pltpu.with_memory_space_constraint(a, pltpu.HBM) for a in arrays]

    operands = pinned(user_factors, item_factors, confidence, pattern, counts.T)
    scratch = [
        pltpu.VMEM(user_factors.shape, BF16),
        pltpu.VMEM(item_factors.shape, BF16),
        pltpu.VMEM(confidence.shape, BF16),
        pltpu.SMEM(pattern.shape, jnp.int32),
        pltpu.SMEM((1, user_tiles), jnp.int32),
        pltpu.VMEM(sums_shape, F32),
        pltpu.VMEM(sums_shape, F32),
        pltpu.SemaphoreType.DMA((4 + user_tiles,)),
    ]

    item_part = pl.pallas_call(
        lambda *refs: item_kernel(item_scales, user_axes, *refs),
        out_shape=pltpu.HBM((item_rows, feat_width), F32),
        in_specs=[in_hbm] * 5,
        out_specs=in_hbm,
        scratch_shapes=scratch + [
            pltpu.VMEM((item_rows, feat_width), F32),
            pltpu.SemaphoreType.DMA((2 * item_tiles,)),
        ],
        compiler_params=params,
        name="item_sums",
    )(*operands)

    keep, send = pl.pallas_call(
        lambda *refs: user_kernel(user_scales, item_axes, *refs),
        out_shape=(pltpu.VMEM((user_rows // 2, feat_width), F32),) * 2,
        in_specs=[in_hbm] * 5,
        out_specs=(in_vmem,) * 2,
        scratch_shapes=scratch,
        compiler_params=params,
        name="user_sums",
    )(*operands)

    def exchange(part, axes):
        size = lax.axis_size(axes)
        moved = lax.all_to_all(part, axes, 0, 0, tiled=True)
        return moved.reshape(size, part.shape[0] // size, feat_width)

    def halve(keep, send, name, distance):
        pairs = [(i, i ^ distance) for i in range(lax.axis_size(name))]
        whole = keep + lax.ppermute(send, name, pairs)
        half = whole.shape[0] // 2
        return whole[:half], whole[half:], whole

    steps = [(name, 2 ** level) for name in ("core", "y") for level in range(lax.axis_size(name).bit_length() - 1)]
    moved = exchange(item_part, ("x", "zl"))
    for step in steps[:-1]:
        keep, send, _ = halve(keep, send, *step)
    moved, keep, send = lax.optimization_barrier((moved, keep, send))
    item_gradient = exchange(moved.sum(0), "zh").sum(0)
    user_gradient = halve(keep, send, *steps[-1])[2]
    return (user_gradient, item_gradient[None])


def solution(mesh):
    fine = Mesh(mesh.devices.reshape(4, 8, 2, 8, 2), USERS + ITEMS)
    return jax.shard_map(
        shards,
        mesh=fine,
        in_specs=(
            P(USERS, None),
            P(ITEMS, None),
            P(USERS, ITEMS, None),
            P(USERS, ITEMS),
            P(USERS, ITEMS, None, None, None),
        ),
        out_specs=(P(USERS + ITEMS, None), P(ITEMS, USERS, None)),
        check_vma=False,
    )
```
